32 devices in a mesh: ens: 2 (over y), tile: 4 (over z), row: 2 (over x), lev: 2 (over core).
Axes of the slice: x: 2, y: 2, z: 4, core: 2. Of those that a mesh axis runs over, the one named last changes fastest.
Arguments:
- air_state: float32 [72, 128, 256], P('lev', ('ens', 'tile'), 'row'), parts along dimension 1, may hold values from -6 to 6
- air_kappa: float32 [128, 256], P(('ens', 'tile'), 'row'), parts along dimension 0, may hold values from 0.05 to 0.24
- air_exchange: float32 [128, 256], P(('ens', 'tile'), 'row'), parts along dimension 0, may hold values from 0.2 to 1.5
- air_weights: float32 [72], P('lev'), may hold values from 0.02 to 0.2
- air_profile: float32 [72], P('lev'), may hold values from 0.005 to 0.05
- sea_state: float32 [80, 128, 256], P('lev', ('ens', 'tile'), 'row'), parts along dimension 1, may hold values from -6 to 6
- sea_kappa: float32 [128, 256], P(('ens', 'tile'), 'row'), parts along dimension 0, may hold values from 0.05 to 0.24
- sea_exchange: float32 [128, 256], P(('ens', 'tile'), 'row'), parts along dimension 0, may hold values from 0.2 to 1
- sea_mask: int32 [128, 256], P(('ens', 'tile'), 'row'), parts along dimension 0, may hold values 0 or 1
- sea_weights: float32 [80], P('lev'), may hold values from 0.02 to 0.2
- sea_profile: float32 [80], P('lev'), may hold values from 0.005 to 0.05
- air_counts: int32 [16, 8], P(('ens', 'tile', 'row')), parts along dimension 0, may hold values from 1 to 32, as said below
- air_send: int32 [16, 8, 32], P(('ens', 'tile', 'row')), parts along dimension 0, may hold values from 0 to 2047
- air_source: int32 [16, 2048], P(('ens', 'tile', 'row')), parts along dimension 0, may hold values from 0 to 255, as said below
- air_target: int32 [16, 2048], P(('ens', 'tile', 'row')), parts along dimension 0, may hold values from 0 to 2047
- air_share: float32 [16, 2048], P(('ens', 'tile', 'row')), parts along dimension 0, may hold values from 0.25 to 1
- sea_counts: int32 [16, 8], P(('ens', 'tile', 'row')), parts along dimension 0, may hold values from 1 to 32, as said below
- sea_send: int32 [16, 8, 32], P(('ens', 'tile', 'row')), parts along dimension 0, may hold values from 0 to 2047
- sea_source: int32 [16, 2048], P(('ens', 'tile', 'row')), parts along dimension 0, may hold values from 0 to 255, as said below
- sea_target: int32 [16, 2048], P(('ens', 'tile', 'row')), parts along dimension 0, may hold values from 0 to 2047
- sea_share: float32 [16, 2048], P(('ens', 'tile', 'row')), parts along dimension 0, may hold values from 0.25 to 1
Outputs:
- air_final: float32 [72, 128, 256], P('lev', ('ens', 'tile'), 'row'), parts along dimension 1
- sea_final: float32 [80, 128, 256], P('lev', ('ens', 'tile'), 'row'), parts along dimension 1
The draws below stay inside these ranges and needn't reach their ends.
There are 2 independent parts, one for each index of `ens`. The reference program is written for one: setup_inputs(seed, part) draws one part's arguments, and reference() takes and returns one part's arrays. A program takes and returns all parts, laid end to end along the dimension named above; an argument that names none is the same for every part. Nothing has to cross between parts.
Inputs may be any that keep to these rules, and one draw needn't show every extreme that they name: `air_counts`: each sending device has 32 live slots to some receiving device; about a quarter of the receiving devices may get up to 32 from each sender, the others at most about two thirds of that. `air_source`: row p names s * 32 + c with c < air_counts[s, p]: only live slots are read. `sea_counts`: each sending device has 32 live slots to some receiving device; about a quarter of the receiving devices may get up to 32 from each sender, the others at most about two thirds of that. `sea_source`: row p names s * 32 + c with c < sea_counts[s, p]: only live slots are read.
All inputs are finite; a program needn't handle non-finite values. No bound on the sum of `sea_mask` on one device may be relied on, other than what follows from the above.
Results may differ from the reference program's by a relative error of at most 0.0001.
Values sent between devices are 32-bit elements; how exact they have to be, the bound alone decides.
A program may use at most 64 MiB of HBM per device.

```python
import math
import jax
import jax.numpy as jnp

KA = 72
KO = 80
AIR_STEPS = 4
SEA_STEPS = 2
CAP = 32
CAX = 16
CAY = 128
COX = 16
COY = 128
PEERS = 8
AX = 64
AY = 256
OX = 64
OY = 256
ER_O = 2048
ER_A = 2048
N_TILE = 4
N_ROW = 2


def coupler_counts(key, offset):
    table_key = jax.random.fold_in(key, offset)
    first_key, second_key = jax.random.split(table_key)
    heavy_peer = jnp.where(jax.random.randint(first_key, (PEERS,), 0, 4) == 3, 3, 2).astype(jnp.int32)
    drawn_slot = jax.random.randint(second_key, (PEERS, PEERS), 0, CAP).astype(jnp.int32)
    counts = 1 + drawn_slot * heavy_peer[None, :] // 3
    senders = jnp.arange(PEERS, dtype=jnp.int32)
    return counts.at[senders, (senders * 5 + 1) % PEERS].set(CAP).astype(jnp.int32)


def coupler_sources(key, offset, entries):
    counts = coupler_counts(key, offset)
    table_key = jax.random.fold_in(key, offset + 100)
    first_key, second_key = jax.random.split(table_key)
    sender = jax.random.randint(first_key, (PEERS, entries), 0, PEERS).astype(jnp.int32)
    drawn_slot = jax.random.randint(second_key, (PEERS, entries), 0, 1048576).astype(jnp.int32)
    receiver = jnp.arange(PEERS, dtype=jnp.int32)[:, None]
    slot_index = drawn_slot % counts[sender, receiver]
    result = (sender * CAP + slot_index).astype(jnp.int32)
    result = result.at[:, 1].set(0)
    last_sender = PEERS - 1
    full_receiver = (last_sender * 5 + 1) % PEERS
    result = result.at[full_receiver, 0].set(last_sender * CAP + CAP - 1)
    return result.astype(jnp.int32)


def draw_air_counts(key, part):
    return coupler_counts(key, 11)


def draw_air_source(key, part):
    return coupler_sources(key, 11, COX * COY)


def draw_sea_counts(key, part):
    return coupler_counts(key, 12)


def draw_sea_source(key, part):
    return coupler_sources(key, 12, CAX * CAY)


def set_ends(values, own_key, least, top_value):
    index_at = [jax.random.randint(jax.random.fold_in(own_key, axis), (), 0, length) for axis, length in enumerate(values.shape)]
    main_axis = values.shape.index(max(values.shape))
    beside = index_at[:main_axis] + [(index_at[main_axis] + 1) % values.shape[main_axis]] + index_at[main_axis + 1:]
    return values.at[tuple(index_at)].set(least).at[tuple(beside)].set(top_value)


def level_of(rng, dims, pieces, low, high):
    level = 1.0
    for dim, blocks in pieces:
        draws = jax.random.uniform(jax.random.fold_in(jax.random.fold_in(rng, 6), dim), (blocks,), jnp.float32, low / len(pieces), high / len(pieces))
        level = level * jnp.repeat(jnp.exp(draws), dims[dim] // blocks).reshape((-1,) + (1,) * (len(dims) - 1 - dim))
    return level


def centred(key, shape, deviation, reach, pieces=(), kind=jnp.bfloat16):
    level = level_of(key, shape, pieces, -0.22, 0.18) if pieces else 1.0
    drawn = jax.random.normal(key, shape, jnp.float32) * deviation * level
    return jnp.minimum(jnp.maximum(drawn, -reach), reach).astype(kind)


def setup_inputs(seed: int = 0, part: int = 0) -> dict:
    seeds = jax.random.split(jax.random.key(seed), 22)
    part_keys = jax.random.split(jax.random.fold_in(seeds[21], part), 22)
    air_state = centred(part_keys[0], (KA, AX, AY), 1.0, 6.0, ((0, 2), (1, 4), (2, 2)), jnp.float32)
    air_kappa = jnp.clip(0.05 + 0.19 * jax.random.uniform(part_keys[1], (AX, AY), jnp.float32) ** level_of(part_keys[1], (AX, AY), ((0, 4), (1, 2)), -0.2, 0.2), 0.05, 0.24)
    air_exchange = jnp.clip(jnp.exp(math.log(1.5) - 2.014903 * jax.random.uniform(part_keys[2], (AX, AY), jnp.float32) ** level_of(part_keys[2], (AX, AY), ((0, 4), (1, 2)), -0.2, 0.2)), 0.2, 1.5)
    air_weights = jnp.clip(jnp.exp(math.log(0.2) - 2.3025851 * jax.random.uniform(seeds[3], (KA,), jnp.float32) ** level_of(seeds[3], (KA,), ((0, 2),), -0.2, 0.2)), 0.02, 0.2)
    air_profile = jnp.clip(jnp.exp(math.log(0.05) - 2.3025851 * jax.random.uniform(seeds[4], (KA,), jnp.float32) ** level_of(seeds[4], (KA,), ((0, 2),), -0.2, 0.2)), 0.005, 0.05)
    sea_state = centred(part_keys[5], (KO, OX, OY), 1.0, 6.0, ((0, 2), (1, 4), (2, 2)), jnp.float32)
    sea_kappa = jnp.clip(0.05 + 0.19 * jax.random.uniform(part_keys[6], (OX, OY), jnp.float32) ** level_of(part_keys[6], (OX, OY), ((0, 4), (1, 2)), -0.2, 0.2), 0.05, 0.24)
    sea_exchange = jnp.clip(jnp.exp(math.log(1.0) - 1.609438 * jax.random.uniform(part_keys[7], (OX, OY), jnp.float32) ** level_of(part_keys[7], (OX, OY), ((0, 4), (1, 2)), -0.2, 0.2)), 0.2, 1.0)
    sea_mask = set_ends((jax.random.randint(part_keys[8], (OX, OY), 0, 4) < 3).astype(jnp.int32), jax.random.fold_in(part_keys[8], 1), 0, 1)
    sea_weights = jnp.clip(jnp.exp(math.log(0.2) - 2.3025851 * jax.random.uniform(seeds[9], (KO,), jnp.float32) ** level_of(seeds[9], (KO,), ((0, 2),), -0.2, 0.2)), 0.02, 0.2)
    sea_profile = jnp.clip(jnp.exp(math.log(0.05) - 2.3025851 * jax.random.uniform(seeds[10], (KO,), jnp.float32) ** level_of(seeds[10], (KO,), ((0, 2),), -0.2, 0.2)), 0.005, 0.05)
    air_counts = draw_air_counts(jax.random.fold_in(jax.random.fold_in(seeds[21], part), 71), part)
    air_send = set_ends(jax.random.randint(part_keys[12], (PEERS, PEERS, CAP), 0, CAX * CAY), jax.random.fold_in(part_keys[12], 1), 0, (CAX * CAY) - 1).astype(jnp.int32)
    air_source = draw_air_source(jax.random.fold_in(jax.random.fold_in(seeds[21], part), 71), part)
    air_target = set_ends(jax.random.randint(part_keys[14], (PEERS, ER_O), 0, COX * COY), jax.random.fold_in(part_keys[14], 1), 0, (COX * COY) - 1).astype(jnp.int32)
    air_share = jnp.clip(0.25 + 0.75 * jax.random.uniform(part_keys[15], (PEERS, ER_O), jnp.float32) ** level_of(part_keys[15], (PEERS, ER_O), ((0, 8),), -0.2, 0.2), 0.25, 1.0)
    sea_counts = draw_sea_counts(jax.random.fold_in(jax.random.fold_in(seeds[21], part), 71), part)
    sea_send = set_ends(jax.random.randint(part_keys[17], (PEERS, PEERS, CAP), 0, COX * COY), jax.random.fold_in(part_keys[17], 1), 0, (COX * COY) - 1).astype(jnp.int32)
    sea_source = draw_sea_source(jax.random.fold_in(jax.random.fold_in(seeds[21], part), 71), part)
    sea_target = set_ends(jax.random.randint(part_keys[19], (PEERS, ER_A), 0, CAX * CAY), jax.random.fold_in(part_keys[19], 1), 0, (CAX * CAY) - 1).astype(jnp.int32)
    sea_share = jnp.clip(0.25 + 0.75 * jax.random.uniform(part_keys[20], (PEERS, ER_A), jnp.float32) ** level_of(part_keys[20], (PEERS, ER_A), ((0, 8),), -0.2, 0.2), 0.25, 1.0)
    return {"air_state": air_state, "air_kappa": air_kappa, "air_exchange": air_exchange, "air_weights": air_weights, "air_profile": air_profile, "sea_state": sea_state, "sea_kappa": sea_kappa, "sea_exchange": sea_exchange, "sea_mask": sea_mask, "sea_weights": sea_weights, "sea_profile": sea_profile, "air_counts": air_counts, "air_send": air_send, "air_source": air_source, "air_target": air_target, "air_share": air_share, "sea_counts": sea_counts, "sea_send": sea_send, "sea_source": sea_source, "sea_target": sea_target, "sea_share": sea_share}


def column_sum(field, weights):
    return jnp.sum(weights[:, None, None] * field, axis=0)


def laplace(field):
    padded = jnp.pad(field, ((0, 0), (1, 1), (1, 1)))
    return padded[:, 2:, 1:-1] + padded[:, :-2, 1:-1] + padded[:, 1:-1, 2:] + padded[:, 1:-1, :-2] - 4.0 * field


def to_blocks(surface, size_x, size_y):
    shaped = surface.reshape(N_TILE, size_x, N_ROW, size_y)
    return jnp.transpose(shaped, (0, 2, 1, 3)).reshape(N_TILE * N_ROW, size_x * size_y)


def from_blocks(blocks, size_x, size_y):
    shaped = blocks.reshape(N_TILE, N_ROW, size_x, size_y)
    return jnp.transpose(shaped, (0, 2, 1, 3)).reshape(N_TILE * size_x, N_ROW * size_y)


def remap(surface, size_x, size_y, counts, send_list, source, target, weight_list, out_x, out_y):
    blocks = to_blocks(surface, size_x, size_y)
    values = jax.vmap(lambda row_values, indices: row_values[indices])(blocks, send_list)
    live_slot = jnp.arange(CAP, dtype=jnp.int32)[None, None, :] < counts[:, :, None]
    buffer = jnp.where(live_slot, values, jnp.zeros_like(values))
    received = jnp.transpose(buffer, (1, 0, 2)).reshape(N_TILE * N_ROW, N_TILE * N_ROW * CAP)
    weighted = jax.vmap(lambda row_values, indices: row_values[indices])(received, source) * weight_list
    summed = jax.vmap(lambda terms, cells: jax.ops.segment_sum(terms, cells, num_segments=out_x * out_y))(weighted, target)
    return from_blocks(summed, out_x, out_y)


def reference(air_state, air_kappa, air_exchange, air_weights, air_profile, sea_state, sea_kappa, sea_exchange, sea_mask, sea_weights, sea_profile, air_counts, air_send, air_source, air_target, air_share, sea_counts, sea_send, sea_source, sea_target, sea_share):
    air_surface = column_sum(air_state, air_weights)
    sea_surface = column_sum(sea_state, sea_weights)
    air_at_sea = remap(air_surface, CAX, CAY, air_counts, air_send, air_source, air_target, air_share, COX, COY)
    sea_at_air = remap(sea_surface, COX, COY, sea_counts, sea_send, sea_source, sea_target, sea_share, CAX, CAY)
    air_field = air_state
    for iteration in range(AIR_STEPS):
        surface = air_surface if iteration == 0 else column_sum(air_field, air_weights)
        air_field = air_field + air_kappa * laplace(air_field) + air_profile[:, None, None] * (air_exchange * (sea_at_air - surface))
    sea_field = sea_state
    land_sea = sea_mask.astype(jnp.float32)
    for iteration in range(SEA_STEPS):
        surface = sea_surface if iteration == 0 else column_sum(sea_field, sea_weights)
        sea_field = sea_field + land_sea * (sea_kappa * laplace(sea_field) + sea_profile[:, None, None] * (sea_exchange * (air_at_sea - surface)))
    return (air_field, sea_field)
```

```python
import functools

import jax
import jax.numpy as jnp
from jax import lax
from jax.experimental import pallas as pl
from jax.experimental.pallas import tpu as pltpu
from jax.sharding import PartitionSpec as P

AIR_STEPS = 4
SEA_STEPS = 2
F32 = jnp.float32
DIRS = tuple((dt, dr) for dt in (-1, 0, 1) for dr in (-1, 0, 1) if (dt, dr) != (0, 0))
LANE = 128
PER = 16


def iota(shape, dim):
    return lax.broadcasted_iota(jnp.int32, shape, dim)


def turn(x, shift, axis):
    return pltpu.roll(x, shift % x.shape[axis], axis)


def lap_wrapped(x):
    return (
        turn(x, 1, 0) + turn(x, -1, 0) + turn(x, 1, 1) + turn(x, -1, 1) - 4.0 * x
    )


def repeat_8(x, low):
    y = jnp.where(low, x, 0.0)
    for width in (8, 16, 32, 64):
        y = y + turn(y, width, 1)
    return y


def kernel(
    n_tile,
    n_row,
    air_ref, ka_ref, ea_ref, aw_ref, ap_ref,
    sea_ref, ko_ref, eo_ref, mask_ref, ow_ref, op_ref,
    acnt_ref, asend_ref, asrc_ref, atgt_ref, ashr_ref,
    ocnt_ref, osend_ref, osrc_ref, otgt_ref, oshr_ref,
    air_out, sea_out,
    ext1, ext2, ext3, rows_send, rows_recv, lev_send, lev_recv,
    slot_send, slot_recv, index_ref, onehot_ref, edge_air, edge_sea,
    send1, recv1, send2, recv2, send3, recv3,
    rs_send, rs_recv, lv_send, lv_recv, sl_send, sl_recv,
):
    t = lax.axis_index("tile")
    r = lax.axis_index("row")
    lev = lax.axis_index("lev")
    me = t * n_row + r
    peers = n_tile * n_row
    n_air = air_ref.shape[0]
    n_sea = sea_ref.shape[0]
    g_air = (n_air + PER - 1) // PER
    g_sea = (n_sea + PER - 1) // PER
    planes = g_air + g_sea
    cap = asend_ref.shape[2]
    entries = asrc_ref.shape[1]
    MESH = pl.DeviceIdType.MESH

    barrier = pltpu.get_barrier_semaphore()

    def greet(p, carry):
        @pl.when(p != me)
        def _():
            pl.semaphore_signal(
                barrier, inc=1, device_id={"tile": p // n_row, "row": p % n_row},
                device_id_type=MESH,
            )
        return carry

    lax.fori_loop(0, peers, greet, 0)
    pl.semaphore_signal(barrier, inc=1, device_id={"lev": 1 - lev}, device_id_type=MESH)

    lane16 = iota((16, LANE), 1)
    group16 = lane16 // 8

    def columns(state_ref, weights_ref, count, base):
        total = jnp.zeros((16, LANE), F32)
        for i in range((count + PER - 1) // PER):
            acc = jnp.zeros((16, LANE), F32)
            for j in range(PER):
                k = i * PER + j
                if k < count:
                    x = state_ref[k]
                    total = total + weights_ref[k] * x
                    acc = jnp.where(group16 == j, turn(x, 8 * j + 4, 1), acc)
            ext1[base + i, 8:24, LANE:2 * LANE] = acc
        return total

    def weight_of_flux(weights_ref, profile_ref, count):
        total = weights_ref[0] * profile_ref[0]
        for k in range(1, count):
            total = total + weights_ref[k] * profile_ref[k]
        return total

    lev_send[0:16, :] = columns(air_ref, aw_ref, n_air, 0)
    lev_send[16:32, :] = columns(sea_ref, ow_ref, n_sea, g_air)
    lev_send[32:40, :] = jnp.zeros((8, LANE), F32) + weight_of_flux(aw_ref, ap_ref, n_air)
    lev_send[40:48, :] = jnp.zeros((8, LANE), F32) + weight_of_flux(ow_ref, op_ref, n_sea)
    land_sea = mask_ref[...].astype(F32)
    ext1[planes, 8:24, LANE:2 * LANE] = ka_ref[...]
    ext1[planes + 1, 8:24, LANE:2 * LANE] = ea_ref[...]
    ext1[planes + 2, 8:24, LANE:2 * LANE] = land_sea * ko_ref[...]
    ext1[planes + 3, 8:24, LANE:2 * LANE] = land_sea * eo_ref[...]

    sub = iota((8, LANE), 0)
    upper = sub < 4

    def pack_rows(state_ref, count, base):
        for j in range(count // 2):
            a, b = state_ref[2 * j], state_ref[2 * j + 1]
            rows_send[0, base + j] = jnp.where(upper, a[0:8], turn(b[0:8], 4, 0))
            rows_send[1, base + j] = jnp.where(upper, turn(a[8:16], 4, 0), b[8:16])

    pack_rows(air_ref, n_air, 0)
    pack_rows(sea_ref, n_sea, n_air // 2)

    def exists(dt, dr):
        ok = jnp.bool_(True)
        if dt < 0:
            ok = ok & (t + dt >= 0)
        if dt > 0:
            ok = ok & (t + dt < n_tile)
        if dr < 0:
            ok = ok & (r + dr >= 0)
        if dr > 0:
            ok = ok & (r + dr < n_row)
        return ok

    def halo_copy(ext, send, recv, d):
        dt, dr = DIRS[d]
        source_rows = {-1: (8, 16), 0: (8, 24), 1: (16, 24)}[dt]
        target_rows = {-1: (24, 32), 0: (8, 24), 1: (0, 8)}[dt]
        target_lanes = {-1: 2 * LANE, 0: LANE, 1: 0}[dr]
        return pltpu.make_async_remote_copy(
            src_ref=ext.at[:, source_rows[0]:source_rows[1], LANE:2 * LANE],
            dst_ref=ext.at[:, target_rows[0]:target_rows[1], target_lanes:target_lanes + LANE],
            send_sem=send.at[d],
            recv_sem=recv.at[d],
            device_id={"tile": t + dt, "row": r + dr},
            device_id_type=MESH,
        )

    def halo_start(ext, send, recv):
        for d, (dt, dr) in enumerate(DIRS):
            @pl.when(exists(dt, dr))
            def _():
                halo_copy(ext, send, recv, d).start()

    def halo_clear(ext):
        for dt, dr in DIRS:
            rows = {-1: (24, 32), 0: (8, 24), 1: (0, 8)}[dt]
            lanes = {-1: 2 * LANE, 0: LANE, 1: 0}[dr]
            @pl.when(jnp.logical_not(exists(-dt, -dr)))
            def _():
                ext[:, rows[0]:rows[1], lanes:lanes + LANE] = jnp.zeros(
                    (ext.shape[0], rows[1] - rows[0], LANE), F32
                )

    def halo_wait_recv(ext, send, recv):
        for d, (dt, dr) in enumerate(DIRS):
            @pl.when(exists(-dt, -dr))
            def _():
                halo_copy(ext, send, recv, d).wait_recv()

    def halo_wait_send(ext, send, recv):
        for d, (dt, dr) in enumerate(DIRS):
            @pl.when(exists(dt, dr))
            def _():
                halo_copy(ext, send, recv, d).wait_send()

    def rows_copy(d):
        return pltpu.make_async_remote_copy(
            src_ref=rows_send.at[d], dst_ref=rows_recv.at[d],
            send_sem=rs_send.at[d], recv_sem=rs_recv.at[d],
            device_id={"tile": t + (1 if d else -1)}, device_id_type=MESH,
        )

    lev_copy = pltpu.make_async_remote_copy(
        src_ref=lev_send, dst_ref=lev_recv, send_sem=lv_send, recv_sem=lv_recv,
        device_id={"lev": 1 - lev}, device_id_type=MESH,
    )

    pl.semaphore_wait(barrier, peers)
    lev_copy.start()
    halo_start(ext1, send1, recv1)
    for d in range(2):
        @pl.when(exists(1 if d else -1, 0))
        def _():
            rows_copy(d).start()

        @pl.when(jnp.logical_not(exists(-1 if d else 1, 0)))
        def _():
            rows_recv[d] = jnp.zeros(rows_recv.shape[1:], F32)
    halo_clear(ext1)
    halo_clear(ext2)
    halo_clear(ext3)

    cells = 16 * LANE
    index_ref[...] = jnp.zeros(index_ref.shape, jnp.int32)
    index_ref[:, 0:cap] = asend_ref[0]
    index_ref[:, cap:2 * cap] = osend_ref[0] + cells
    index = index_ref[...]
    on_diagonal = iota((peers, peers), 0) == iota((peers, peers), 1)

    def live_count(counts_ref):
        counts = jnp.broadcast_to(counts_ref[...].astype(F32), (peers, peers))
        return jnp.sum(jnp.where(on_diagonal, counts, 0.0), axis=1, keepdims=True)

    slot_lane = iota((peers, LANE), 1)
    limit = jnp.where(slot_lane < cap, live_count(acnt_ref), live_count(ocnt_ref))
    limit = jnp.where(slot_lane < 2 * cap, limit, 0.0)
    live = (slot_lane % cap).astype(F32) < limit
    index_lane = index % LANE
    index_row = index // LANE

    lev_copy.wait_recv()
    surface = lev_send[...] + lev_recv[...]
    ext2[0, 8:24, LANE:2 * LANE] = surface[0:16]
    ext2[1, 8:24, LANE:2 * LANE] = surface[16:32]
    values = jnp.zeros((peers, LANE), F32)
    for x in range(32):
        row = jnp.broadcast_to(surface[x:x + 1], (peers, LANE))
        picked = jnp.take_along_axis(row, index_lane, axis=1, mode="promise_in_bounds")
        values = jnp.where(index_row == x, picked, values)
    values = jnp.where(live, values, 0.0)
    slot_send[...] = values.reshape(peers, 1, LANE)

    def slot_copy(p, recv_slot):
        return pltpu.make_async_remote_copy(
            src_ref=slot_send.at[p], dst_ref=slot_recv.at[recv_slot],
            send_sem=sl_send.at[p], recv_sem=sl_recv.at[recv_slot],
            device_id={"tile": p // n_row, "row": p % n_row}, device_id_type=MESH,
        )

    def others(action):
        def step(p, carry):
            @pl.when(p != me)
            def _():
                action(p)
            return carry
        lax.fori_loop(0, peers, step, 0)

    others(lambda p: slot_copy(p, me).start())
    halo_start(ext2, send2, recv2)
    slot_recv[me] = slot_send[me]

    cell_y = iota((LANE, LANE), 0)
    for m, tgt_ref in enumerate((atgt_ref, otgt_ref)):
        for c in range(entries // LANE):
            y = tgt_ref[0:1, c * LANE:(c + 1) * LANE] % LANE
            onehot_ref[m, :, c * LANE:(c + 1) * LANE] = jnp.where(
                jnp.broadcast_to(y, (LANE, LANE)) == cell_y, 1.0, 0.0
            ).astype(jnp.bfloat16)

    others(lambda p: slot_copy(p, p).wait_recv())
    table = slot_recv[...].reshape(peers, LANE)
    cell_x = iota((16, LANE), 0)
    sender = iota((peers, LANE), 0)
    for m, (src_ref, tgt_ref, shr_ref) in enumerate(
        ((asrc_ref, atgt_ref, ashr_ref), (osrc_ref, otgt_ref, oshr_ref))
    ):
        parts = ([], [], [])
        for c in range(entries // LANE):
            at = slice(c * LANE, (c + 1) * LANE)
            source = jnp.broadcast_to(src_ref[0:1, at], (peers, LANE))
            picked = jnp.take_along_axis(
                table, source % cap + m * cap, axis=1, mode="promise_in_bounds"
            )
            value = jnp.sum(jnp.where(source // cap == sender, picked, 0.0), axis=0, keepdims=True)
            value = value * shr_ref[0:1, at]
            x = jnp.broadcast_to(tgt_ref[0:1, at] // LANE, (16, LANE))
            spread = jnp.where(x == cell_x, jnp.broadcast_to(value, (16, LANE)), 0.0)
            high = spread.astype(jnp.bfloat16)
            rest = spread - high.astype(F32)
            middle = rest.astype(jnp.bfloat16)
            low = (rest - middle.astype(F32)).astype(jnp.bfloat16)
            parts[0].append(high)
            parts[1].append(middle)
            parts[2].append(low)
        left = jnp.concatenate([jnp.concatenate(p, axis=1) for p in parts], axis=0)
        product = lax.dot_general(
            left, onehot_ref[m], (((1,), (1,)), ((), ())), preferred_element_type=F32
        )
        ext3[1 - m, 8:24, LANE:2 * LANE] = product[0:16] + product[16:32] + product[32:48]
    halo_start(ext3, send3, recv3)

    halo_wait_recv(ext1, send1, recv1)
    for d in range(2):
        @pl.when(exists(-1 if d else 1, 0))
        def _():
            rows_copy(d).wait_recv()

    lane32 = iota((32, LANE), 1)
    low_lanes = lane32 < 8
    left_half = lane32 % 8 < 4
    first_lane = lane32 == 0
    last_lane = lane32 == LANE - 1

    def advance(state_ref, out_ref, edge_ref, count, base, rows_base, plane, steps):
        kl = repeat_8(turn(ext1[plane, :, 0:LANE], 4, 1), low_lanes)
        kc = repeat_8(turn(ext1[plane, :, LANE:2 * LANE], 4, 1), low_lanes)
        kr = repeat_8(turn(ext1[plane, :, 2 * LANE:], 4, 1), low_lanes)
        kappa_left = jnp.where(left_half, kl, kc)
        kappa_right = jnp.where(left_half, kc, kr)
        kappa = ext1[plane, :, LANE:2 * LANE]
        for i in range((count + PER - 1) // PER):
            own = ext1[base + i, :, LANE:2 * LANE]
            left = jnp.where(left_half, ext1[base + i, :, 0:LANE], own)
            right = jnp.where(left_half, own, ext1[base + i, :, 2 * LANE:])
            for n in range(steps):
                edge_ref[n, i] = jnp.where(lane32 % 8 == 3, left, turn(right, -2, 1))
                if n + 1 < steps:
                    left = left + kappa_left * lap_wrapped(left)
                    right = right + kappa_right * lap_wrapped(right)

        def pair(q, carry):
            top, bottom = rows_recv[1, rows_base + q], rows_recv[0, rows_base + q]
            for b in range(2):
                k = 2 * q + b
                i, j = k // PER, k % PER
                above = top if b else turn(top, 4, 0)
                below = turn(bottom, 4, 0) if b else bottom
                x = jnp.concatenate([above, state_ref[k], below], axis=0)
                for n in range(steps):
                    edge = pltpu.roll(edge_ref[n, i], (2 * LANE - 3 - 8 * j) % LANE, 1)
                    around = (
                        turn(x, 1, 0) + turn(x, -1, 0)
                        + jnp.where(first_lane, edge, turn(x, 1, 1))
                        + jnp.where(last_lane, edge, turn(x, -1, 1))
                    )
                    x = x + kappa * (around - 4.0 * x)
                out_ref[k] = x[8:24]
            return carry

        lax.fori_loop(0, count // 2, pair, 0)

    advance(air_ref, air_out, edge_air, n_air, 0, 0, planes, AIR_STEPS)
    advance(sea_ref, sea_out, edge_sea, n_sea, g_air, n_air // 2, planes + 2, SEA_STEPS)

    halo_wait_recv(ext2, send2, recv2)
    halo_wait_recv(ext3, send3, recv3)
    for m, (out_ref, profile_ref, count, steps) in enumerate(
        ((air_out, ap_ref, n_air, AIR_STEPS), (sea_out, op_ref, n_sea, SEA_STEPS))
    ):
        flux_weight = surface[32 + 8 * m:33 + 8 * m]
        flux_weight = jnp.concatenate([flux_weight] * 3, axis=1)
        kappa = ext1[planes + 2 * m]
        exchange = ext1[planes + 2 * m + 1]
        s = ext2[m]
        q = ext3[m]
        g = None
        for n in range(steps):
            flux = exchange * (q - s)
            g = flux if g is None else g + kappa * lap_wrapped(g) + flux
            if n + 1 < steps:
                s = s + kappa * lap_wrapped(s) + flux_weight * flux
        center = g[8:24, LANE:2 * LANE]
        for k in range(count):
            out_ref[k] = out_ref[k] + profile_ref[k] * center

    lev_copy.wait_send()
    others(lambda p: slot_copy(p, me).wait_send())
    halo_wait_send(ext1, send1, recv1)
    halo_wait_send(ext2, send2, recv2)
    halo_wait_send(ext3, send3, recv3)
    for d in range(2):
        @pl.when(exists(1 if d else -1, 0))
        def _():
            rows_copy(d).wait_send()


def body(*args):
    air, sea = args[0], args[5]
    n_air, n_sea = air.shape[0], sea.shape[0]
    n_tile, n_row = lax.axis_size("tile"), lax.axis_size("row")
    peers = n_tile * n_row
    entries = args[13].shape[1]
    g_air, g_sea = -(-n_air // PER), -(-n_sea // PER)
    vmem = pl.BlockSpec(memory_space=pltpu.VMEM)
    smem = pl.BlockSpec(memory_space=pltpu.SMEM)
    scalars = (3, 4, 9, 10)
    packed = (n_air + n_sea) // 2
    DMA = pltpu.SemaphoreType.DMA
    return pl.pallas_call(
        functools.partial(kernel, n_tile, n_row),
        out_shape=(
            jax.ShapeDtypeStruct(air.shape, F32),
            jax.ShapeDtypeStruct(sea.shape, F32),
        ),
        in_specs=[smem if i in scalars else vmem for i in range(len(args))],
        out_specs=(vmem, vmem),
        scratch_shapes=[
            pltpu.VMEM((g_air + g_sea + 4, 32, 3 * LANE), F32),
            pltpu.VMEM((2, 32, 3 * LANE), F32),
            pltpu.VMEM((2, 32, 3 * LANE), F32),
            pltpu.VMEM((2, packed, 8, LANE), F32),
            pltpu.VMEM((2, packed, 8, LANE), F32),
            pltpu.VMEM((48, LANE), F32),
            pltpu.VMEM((48, LANE), F32),
            pltpu.VMEM((peers, 1, LANE), F32),
            pltpu.VMEM((peers, 1, LANE), F32),
            pltpu.VMEM((peers, LANE), jnp.int32),
            pltpu.VMEM((2, LANE, entries), jnp.bfloat16),
            pltpu.VMEM((AIR_STEPS, g_air, 32, LANE), F32),
            pltpu.VMEM((SEA_STEPS, g_sea, 32, LANE), F32),
            DMA((8,)), DMA((8,)), DMA((8,)), DMA((8,)), DMA((8,)), DMA((8,)),
            DMA((2,)), DMA((2,)), DMA, DMA, DMA((peers,)), DMA((peers,)),
        ],
        compiler_params=pltpu.CompilerParams(
            collective_id=0, has_side_effects=True, vmem_limit_bytes=32 * 1024 * 1024
        ),
    )(*args)


def solution(mesh):
    field = P("lev", ("ens", "tile"), "row")
    cell = P(("ens", "tile"), "row")
    level = P("lev")
    table = P(("ens", "tile", "row"), None)
    lists = P(("ens", "tile", "row"), None, None)
    placed = (
        field, cell, cell, level, level,
        field, cell, cell, cell, level, level,
        table, lists, table, table, table,
        table, lists, table, table, table,
    )
    return jax.shard_map(
        body, mesh=mesh, in_specs=placed, out_specs=(field, field), check_vma=False
    )
```

```python
import functools

import jax
import jax.numpy as jnp
from jax import lax
from jax.experimental import pallas as pl
from jax.experimental.pallas import tpu as pltpu
from jax.sharding import PartitionSpec as P

AIR_STEPS = 4
SEA_STEPS = 2
F32 = jnp.float32
DIRS = tuple((dt, dr) for dt in (-1, 0, 1) for dr in (-1, 0, 1) if (dt, dr) != (0, 0))
LANE = 128
FIRST = (0, 5, 3, 9)
SECOND = (1, 2, 4, 6, 7, 8, 10, 11, 12, 13, 14, 15, 16, 17, 18, 19, 20)
PER = 16


def iota(shape, dim):
    return lax.broadcasted_iota(jnp.int32, shape, dim)


def turn(x, shift, axis):
    return pltpu.roll(x, shift % x.shape[axis], axis)


def lap_wrapped(x):
    return (
        turn(x, 1, 0) + turn(x, -1, 0) + turn(x, 1, 1) + turn(x, -1, 1) - 4.0 * x
    )


def repeat_8(x, low):
    y = jnp.where(low, x, 0.0)
    for width in (8, 16, 32, 64):
        y = y + turn(y, width, 1)
    return y


def kernel(n_tile, n_row, *refs):
    operands, (air_out, sea_out) = refs[:21], refs[21:23]
    held, rest = refs[23:44], refs[44:]
    (
        air_ref, ka_ref, ea_ref, aw_ref, ap_ref,
        sea_ref, ko_ref, eo_ref, mask_ref, ow_ref, op_ref,
        acnt_ref, asend_ref, asrc_ref, atgt_ref, ashr_ref,
        ocnt_ref, osend_ref, osrc_ref, otgt_ref, oshr_ref,
    ) = held
    (
        in_sem,
        ext1, ext2, ext3, rows_send, rows_recv, lev_send, lev_recv,
        slot_send, slot_recv, index_ref, onehot_ref, edge_air, edge_sea,
        send1, recv1, send2, recv2, send3, recv3,
        rs_send, rs_recv, lv_send, lv_recv, sl_send, sl_recv,
    ) = rest

    def fetch(i):
        return pltpu.make_async_copy(operands[i], held[i], in_sem.at[i])

    for i in FIRST + SECOND:
        fetch(i).start()

    t = lax.axis_index("tile")
    r = lax.axis_index("row")
    lev = lax.axis_index("lev")
    me = t * n_row + r
    peers = n_tile * n_row
    n_air = air_ref.shape[0]
    n_sea = sea_ref.shape[0]
    g_air = (n_air + PER - 1) // PER
    g_sea = (n_sea + PER - 1) // PER
    planes = g_air + g_sea
    cap = asend_ref.shape[2]
    entries = asrc_ref.shape[1]
    MESH = pl.DeviceIdType.MESH

    barrier = pltpu.get_barrier_semaphore()

    def greet(p, carry):
        @pl.when(p != me)
        def _():
            pl.semaphore_signal(
                barrier, inc=1, device_id={"tile": p // n_row, "row": p % n_row},
                device_id_type=MESH,
            )
        return carry

    lax.fori_loop(0, peers, greet, 0)
    pl.semaphore_signal(barrier, inc=1, device_id={"lev": 1 - lev}, device_id_type=MESH)

    lane16 = iota((16, LANE), 1)
    group16 = lane16 // 8

    def column_sum(state_ref, weights_ref, count):
        totals = [weights_ref[k] * state_ref[k] for k in range(4)]
        for k in range(4, count):
            totals[k % 4] = totals[k % 4] + weights_ref[k] * state_ref[k]
        return (totals[0] + totals[1]) + (totals[2] + totals[3])

    def strips(state_ref, count, base):
        for i in range((count + PER - 1) // PER):
            acc = jnp.zeros((16, LANE), F32)
            for j in range(PER):
                k = i * PER + j
                if k < count:
                    acc = jnp.where(group16 == j, turn(state_ref[k], 8 * j + 4, 1), acc)
            ext1[base + i, 8:24, LANE:2 * LANE] = acc

    def weight_of_flux(weights_ref, profile_ref, count):
        total = weights_ref[0] * profile_ref[0]
        for k in range(1, count):
            total = total + weights_ref[k] * profile_ref[k]
        return total

    lev_copy = pltpu.make_async_remote_copy(
        src_ref=lev_send, dst_ref=lev_recv, send_sem=lv_send, recv_sem=lv_recv,
        device_id={"lev": 1 - lev}, device_id_type=MESH,
    )
    for i in FIRST:
        fetch(i).wait()
    lev_send[0:16, :] = column_sum(air_ref, aw_ref, n_air)
    lev_send[16:32, :] = column_sum(sea_ref, ow_ref, n_sea)
    for i in SECOND:
        fetch(i).wait()
    lev_send[32:40, :] = jnp.zeros((8, LANE), F32) + weight_of_flux(aw_ref, ap_ref, n_air)
    lev_send[40:48, :] = jnp.zeros((8, LANE), F32) + weight_of_flux(ow_ref, op_ref, n_sea)
    pl.semaphore_wait(barrier, peers)
    lev_copy.start()

    strips(air_ref, n_air, 0)
    strips(sea_ref, n_sea, g_air)
    land_sea = mask_ref[...].astype(F32)
    ext1[planes, 8:24, LANE:2 * LANE] = ka_ref[...]
    ext1[planes + 1, 8:24, LANE:2 * LANE] = ea_ref[...]
    ext1[planes + 2, 8:24, LANE:2 * LANE] = land_sea * ko_ref[...]
    ext1[planes + 3, 8:24, LANE:2 * LANE] = land_sea * eo_ref[...]

    sub = iota((8, LANE), 0)
    upper = sub < 4

    def pack_rows(state_ref, count, base):
        for j in range(count // 2):
            a, b = state_ref[2 * j], state_ref[2 * j + 1]
            rows_send[0, base + j] = jnp.where(upper, a[0:8], turn(b[0:8], 4, 0))
            rows_send[1, base + j] = jnp.where(upper, turn(a[8:16], 4, 0), b[8:16])

    def exists(dt, dr):
        ok = jnp.bool_(True)
        if dt < 0:
            ok = ok & (t + dt >= 0)
        if dt > 0:
            ok = ok & (t + dt < n_tile)
        if dr < 0:
            ok = ok & (r + dr >= 0)
        if dr > 0:
            ok = ok & (r + dr < n_row)
        return ok

    def halo_copy(ext, send, recv, d):
        dt, dr = DIRS[d]
        source_rows = {-1: (8, 16), 0: (8, 24), 1: (16, 24)}[dt]
        target_rows = {-1: (24, 32), 0: (8, 24), 1: (0, 8)}[dt]
        target_lanes = {-1: 2 * LANE, 0: LANE, 1: 0}[dr]
        return pltpu.make_async_remote_copy(
            src_ref=ext.at[:, source_rows[0]:source_rows[1], LANE:2 * LANE],
            dst_ref=ext.at[:, target_rows[0]:target_rows[1], target_lanes:target_lanes + LANE],
            send_sem=send.at[d],
            recv_sem=recv.at[d],
            device_id={"tile": t + dt, "row": r + dr},
            device_id_type=MESH,
        )

    def halo_start(ext, send, recv):
        for d, (dt, dr) in enumerate(DIRS):
            @pl.when(exists(dt, dr))
            def _():
                halo_copy(ext, send, recv, d).start()

    def halo_clear(ext):
        for dt, dr in DIRS:
            rows = {-1: (24, 32), 0: (8, 24), 1: (0, 8)}[dt]
            lanes = {-1: 2 * LANE, 0: LANE, 1: 0}[dr]
            @pl.when(jnp.logical_not(exists(-dt, -dr)))
            def _():
                ext[:, rows[0]:rows[1], lanes:lanes + LANE] = jnp.zeros(
                    (ext.shape[0], rows[1] - rows[0], LANE), F32
                )

    def halo_wait_recv(ext, send, recv):
        for d, (dt, dr) in enumerate(DIRS):
            @pl.when(exists(-dt, -dr))
            def _():
                halo_copy(ext, send, recv, d).wait_recv()

    def halo_wait_send(ext, send, recv):
        for d, (dt, dr) in enumerate(DIRS):
            @pl.when(exists(dt, dr))
            def _():
                halo_copy(ext, send, recv, d).wait_send()

    def rows_copy(d):
        return pltpu.make_async_remote_copy(
            src_ref=rows_send.at[d], dst_ref=rows_recv.at[d],
            send_sem=rs_send.at[d], recv_sem=rs_recv.at[d],
            device_id={"tile": t + (1 if d else -1)}, device_id_type=MESH,
        )

    halo_start(ext1, send1, recv1)
    pack_rows(air_ref, n_air, 0)
    pack_rows(sea_ref, n_sea, n_air // 2)
    for d in range(2):
        @pl.when(exists(1 if d else -1, 0))
        def _():
            rows_copy(d).start()

        @pl.when(jnp.logical_not(exists(-1 if d else 1, 0)))
        def _():
            rows_recv[d] = jnp.zeros(rows_recv.shape[1:], F32)
    halo_clear(ext1)
    halo_clear(ext2)
    halo_clear(ext3)

    cells = 16 * LANE
    index_ref[...] = jnp.zeros(index_ref.shape, jnp.int32)
    index_ref[:, 0:cap] = asend_ref[0]
    index_ref[:, cap:2 * cap] = osend_ref[0] + cells
    index = index_ref[...]
    on_diagonal = iota((peers, peers), 0) == iota((peers, peers), 1)

    def live_count(counts_ref):
        counts = jnp.broadcast_to(counts_ref[...].astype(F32), (peers, peers))
        return jnp.sum(jnp.where(on_diagonal, counts, 0.0), axis=1, keepdims=True)

    slot_lane = iota((peers, LANE), 1)
    limit = jnp.where(slot_lane < cap, live_count(acnt_ref), live_count(ocnt_ref))
    limit = jnp.where(slot_lane < 2 * cap, limit, 0.0)
    live = (slot_lane % cap).astype(F32) < limit
    index_lane = index % LANE
    index_row = index // LANE

    lev_copy.wait_recv()
    surface = lev_send[...] + lev_recv[...]
    ext2[0, 8:24, LANE:2 * LANE] = surface[0:16]
    ext2[1, 8:24, LANE:2 * LANE] = surface[16:32]
    values = jnp.zeros((peers, LANE), F32)
    for x in range(32):
        row = jnp.broadcast_to(surface[x:x + 1], (peers, LANE))
        picked = jnp.take_along_axis(row, index_lane, axis=1, mode="promise_in_bounds")
        values = jnp.where(index_row == x, picked, values)
    values = jnp.where(live, values, 0.0)
    slot_send[...] = values.reshape(peers, 1, LANE)

    def slot_copy(p, recv_slot):
        return pltpu.make_async_remote_copy(
            src_ref=slot_send.at[p], dst_ref=slot_recv.at[recv_slot],
            send_sem=sl_send.at[p], recv_sem=sl_recv.at[recv_slot],
            device_id={"tile": p // n_row, "row": p % n_row}, device_id_type=MESH,
        )

    def others(action):
        def step(p, carry):
            @pl.when(p != me)
            def _():
                action(p)
            return carry
        lax.fori_loop(0, peers, step, 0)

    others(lambda p: slot_copy(p, me).start())
    halo_start(ext2, send2, recv2)
    slot_recv[me] = slot_send[me]

    cell_y = iota((LANE, LANE), 0)
    for m, tgt_ref in enumerate((atgt_ref, otgt_ref)):
        for c in range(entries // LANE):
            y = tgt_ref[0:1, c * LANE:(c + 1) * LANE] % LANE
            onehot_ref[m, :, c * LANE:(c + 1) * LANE] = jnp.where(
                jnp.broadcast_to(y, (LANE, LANE)) == cell_y, 1.0, 0.0
            ).astype(jnp.bfloat16)

    others(lambda p: slot_copy(p, p).wait_recv())
    table = slot_recv[...].reshape(peers, LANE)
    cell_x = iota((16, LANE), 0)
    sender = iota((peers, LANE), 0)
    for m, (src_ref, tgt_ref, shr_ref) in enumerate(
        ((asrc_ref, atgt_ref, ashr_ref), (osrc_ref, otgt_ref, oshr_ref))
    ):
        parts = ([], [], [])
        for c in range(entries // LANE):
            at = slice(c * LANE, (c + 1) * LANE)
            source = jnp.broadcast_to(src_ref[0:1, at], (peers, LANE))
            picked = jnp.take_along_axis(
                table, source % cap + m * cap, axis=1, mode="promise_in_bounds"
            )
            value = jnp.sum(jnp.where(source // cap == sender, picked, 0.0), axis=0, keepdims=True)
            value = value * shr_ref[0:1, at]
            x = jnp.broadcast_to(tgt_ref[0:1, at] // LANE, (16, LANE))
            spread = jnp.where(x == cell_x, jnp.broadcast_to(value, (16, LANE)), 0.0)
            high = spread.astype(jnp.bfloat16)
            rest = spread - high.astype(F32)
            middle = rest.astype(jnp.bfloat16)
            low = (rest - middle.astype(F32)).astype(jnp.bfloat16)
            parts[0].append(high)
            parts[1].append(middle)
            parts[2].append(low)
        left = jnp.concatenate([jnp.concatenate(p, axis=1) for p in parts], axis=0)
        product = lax.dot_general(
            left, onehot_ref[m], (((1,), (1,)), ((), ())), preferred_element_type=F32
        )
        ext3[1 - m, 8:24, LANE:2 * LANE] = product[0:16] + product[16:32] + product[32:48]
    halo_start(ext3, send3, recv3)

    halo_wait_recv(ext1, send1, recv1)
    for d in range(2):
        @pl.when(exists(-1 if d else 1, 0))
        def _():
            rows_copy(d).wait_recv()

    lane32 = iota((32, LANE), 1)
    low_lanes = lane32 < 8
    left_half = lane32 % 8 < 4
    lane24 = iota((24, LANE), 1)
    first_lane = lane24 == 0
    last_lane = lane24 == LANE - 1

    def advance(state_ref, out_ref, edge_ref, count, base, rows_base, plane, steps):
        kl = repeat_8(turn(ext1[plane, :, 0:LANE], 4, 1), low_lanes)
        kc = repeat_8(turn(ext1[plane, :, LANE:2 * LANE], 4, 1), low_lanes)
        kr = repeat_8(turn(ext1[plane, :, 2 * LANE:], 4, 1), low_lanes)
        kappa_left = jnp.where(left_half, kl, kc)
        kappa_right = jnp.where(left_half, kc, kr)
        kappa = ext1[plane, 4:28, LANE:2 * LANE]
        for i in range((count + PER - 1) // PER):
            own = ext1[base + i, :, LANE:2 * LANE]
            left = jnp.where(left_half, ext1[base + i, :, 0:LANE], own)
            right = jnp.where(left_half, own, ext1[base + i, :, 2 * LANE:])
            for n in range(steps):
                edge = jnp.where(lane32 % 8 == 3, left, turn(right, -2, 1))
                edge_ref[n, i] = edge[4:28]
                if n + 1 < steps:
                    left = left + kappa_left * lap_wrapped(left)
                    right = right + kappa_right * lap_wrapped(right)

        def group(h, carry):
            fields, places = [], []
            for b in range(levels):
                k = h * levels + b
                q = k // 2
                top, bottom = rows_recv[1, rows_base + q], rows_recv[0, rows_base + q]
                if b % 2:
                    top = turn(top, 4, 0)
                else:
                    bottom = turn(bottom, 4, 0)
                a = turn(state_ref[k, 0:8, :], 4, 0)
                c = turn(state_ref[k, 8:16, :], 4, 0)
                fields.append(jnp.concatenate(
                    [jnp.where(upper, top, a), jnp.where(upper, a, c), jnp.where(upper, c, bottom)],
                    axis=0,
                ))
                places.append((k // PER, (2 * LANE - 3 - 8 * (k % PER)) % LANE))
            for n in range(steps):
                for b in range(levels):
                    x = fields[b]
                    i, shift = places[b]
                    edge = pltpu.roll(edge_ref[n, i], shift, 1)
                    around = (
                        turn(x, 1, 0) + turn(x, -1, 0)
                        + jnp.where(first_lane, edge, turn(x, 1, 1))
                        + jnp.where(last_lane, edge, turn(x, -1, 1))
                    )
                    fields[b] = x + kappa * (around - 4.0 * x)
            for b in range(levels):
                x = fields[b]
                k = h * levels + b
                a, c, e = turn(x[0:8], 4, 0), turn(x[8:16], 4, 0), turn(x[16:24], 4, 0)
                out_ref[k, 0:8, :] = jnp.where(upper, a, c)
                out_ref[k, 8:16, :] = jnp.where(upper, c, e)
            return carry

        levels = max(v for v in (2, 4, 6, 8) if count % v == 0)
        lax.fori_loop(0, count // levels, group, 0)

    advance(air_ref, air_out, edge_air, n_air, 0, 0, planes, AIR_STEPS)
    advance(sea_ref, sea_out, edge_sea, n_sea, g_air, n_air // 2, planes + 2, SEA_STEPS)

    halo_wait_recv(ext2, send2, recv2)
    halo_wait_recv(ext3, send3, recv3)
    for m, (out_ref, profile_ref, count, steps) in enumerate(
        ((air_out, ap_ref, n_air, AIR_STEPS), (sea_out, op_ref, n_sea, SEA_STEPS))
    ):
        flux_weight = surface[32 + 8 * m:33 + 8 * m]
        flux_weight = jnp.concatenate([flux_weight] * 3, axis=1)
        kappa = ext1[planes + 2 * m]
        exchange = ext1[planes + 2 * m + 1]
        s = ext2[m]
        q = ext3[m]
        g = None
        for n in range(steps):
            flux = exchange * (q - s)
            g = flux if g is None else g + kappa * lap_wrapped(g) + flux
            if n + 1 < steps:
                s = s + kappa * lap_wrapped(s) + flux_weight * flux
        center = g[8:24, LANE:2 * LANE]
        for k in range(count):
            out_ref[k] = out_ref[k] + profile_ref[k] * center

    lev_copy.wait_send()
    others(lambda p: slot_copy(p, me).wait_send())
    halo_wait_send(ext1, send1, recv1)
    halo_wait_send(ext2, send2, recv2)
    halo_wait_send(ext3, send3, recv3)
    for d in range(2):
        @pl.when(exists(1 if d else -1, 0))
        def _():
            rows_copy(d).wait_send()


def body(*args):
    air, sea = args[0], args[5]
    n_air, n_sea = air.shape[0], sea.shape[0]
    n_tile, n_row = lax.axis_size("tile"), lax.axis_size("row")
    peers = n_tile * n_row
    entries = args[13].shape[1]
    g_air, g_sea = -(-n_air // PER), -(-n_sea // PER)
    vmem = pl.BlockSpec(memory_space=pltpu.VMEM)
    hbm = pl.BlockSpec(memory_space=pltpu.HBM)
    scalars = (3, 4, 9, 10)
    packed = (n_air + n_sea) // 2
    DMA = pltpu.SemaphoreType.DMA
    return pl.pallas_call(
        functools.partial(kernel, n_tile, n_row),
        out_shape=(
            jax.ShapeDtypeStruct(air.shape, F32),
            jax.ShapeDtypeStruct(sea.shape, F32),
        ),
        in_specs=[hbm] * len(args),
        out_specs=(vmem, vmem),
        scratch_shapes=[
            (pltpu.SMEM if i in scalars else pltpu.VMEM)(v.shape, v.dtype)
            for i, v in enumerate(args)
        ] + [
            DMA((len(args),)),
            pltpu.VMEM((g_air + g_sea + 4, 32, 3 * LANE), F32),
            pltpu.VMEM((2, 32, 3 * LANE), F32),
            pltpu.VMEM((2, 32, 3 * LANE), F32),
            pltpu.VMEM((2, packed, 8, LANE), F32),
            pltpu.VMEM((2, packed, 8, LANE), F32),
            pltpu.VMEM((48, LANE), F32),
            pltpu.VMEM((48, LANE), F32),
            pltpu.VMEM((peers, 1, LANE), F32),
            pltpu.VMEM((peers, 1, LANE), F32),
            pltpu.VMEM((peers, LANE), jnp.int32),
            pltpu.VMEM((2, LANE, entries), jnp.bfloat16),
            pltpu.VMEM((AIR_STEPS, g_air, 24, LANE), F32),
            pltpu.VMEM((SEA_STEPS, g_sea, 24, LANE), F32),
            DMA((8,)), DMA((8,)), DMA((8,)), DMA((8,)), DMA((8,)), DMA((8,)),
            DMA((2,)), DMA((2,)), DMA, DMA, DMA((peers,)), DMA((peers,)),
        ],
        compiler_params=pltpu.CompilerParams(
            collective_id=0, has_side_effects=True, vmem_limit_bytes=32 * 1024 * 1024
        ),
    )(*args)


def solution(mesh):
    field = P("lev", ("ens", "tile"), "row")
    cell = P(("ens", "tile"), "row")
    level = P("lev")
    table = P(("ens", "tile", "row"), None)
    lists = P(("ens", "tile", "row"), None, None)
    placed = (
        field, cell, cell, level, level,
        field, cell, cell, cell, level, level,
        table, lists, table, table, table,
        table, lists, table, table, table,
    )
    return jax.shard_map(
        body, mesh=mesh, in_specs=placed, out_specs=(field, field), check_vma=False
    )
```

```python
import functools

import jax
import jax.numpy as jnp
from jax import lax
from jax.experimental import pallas as pl
from jax.experimental.pallas import tpu as pltpu
from jax.sharding import PartitionSpec as P

AIR_STEPS = 4
SEA_STEPS = 2
F32 = jnp.float32
DIRS = tuple((dt, dr) for dt in (-1, 0, 1) for dr in (-1, 0, 1) if (dt, dr) != (0, 0))
LANE = 128
FIRST = (0, 5, 3, 9)
SECOND = (1, 2, 4, 6, 7, 8, 10, 11, 12, 13, 14, 15, 16, 17, 18, 19, 20)
PER = 16


def iota(shape, dim):
    return lax.broadcasted_iota(jnp.int32, shape, dim)


def turn(x, shift, axis):
    return pltpu.roll(x, shift % x.shape[axis], axis)


def lap_wrapped(x):
    return (
        turn(x, 1, 0) + turn(x, -1, 0) + turn(x, 1, 1) + turn(x, -1, 1) - 4.0 * x
    )


def repeat_8(x, low):
    y = jnp.where(low, x, 0.0)
    for width in (8, 16, 32, 64):
        y = y + turn(y, width, 1)
    return y


def kernel(n_tile, n_row, *refs):
    operands, (air_out, sea_out) = refs[:21], refs[21:23]
    held, rest = refs[23:44], refs[44:]
    (
        air_ref, ka_ref, ea_ref, aw_ref, ap_ref,
        sea_ref, ko_ref, eo_ref, mask_ref, ow_ref, op_ref,
        acnt_ref, asend_ref, asrc_ref, atgt_ref, ashr_ref,
        ocnt_ref, osend_ref, osrc_ref, otgt_ref, oshr_ref,
    ) = held
    (
        in_sem,
        ext1, ext2, ext3, rows_send, rows_recv, lev_send, lev_recv,
        slot_send, slot_recv, index_ref, onehot_ref, edge_air, edge_sea,
        send1, recv1, send2, recv2, send3, recv3,
        rs_send, rs_recv, lv_send, lv_recv, sl_send, sl_recv,
    ) = rest

    def fetch(i):
        return pltpu.make_async_copy(operands[i], held[i], in_sem.at[i])

    for i in FIRST + SECOND:
        fetch(i).start()

    t = lax.axis_index("tile")
    r = lax.axis_index("row")
    lev = lax.axis_index("lev")
    me = t * n_row + r
    peers = n_tile * n_row
    n_air = air_ref.shape[0]
    n_sea = sea_ref.shape[0]
    g_air = (n_air + PER - 1) // PER
    g_sea = (n_sea + PER - 1) // PER
    planes = g_air + g_sea
    cap = asend_ref.shape[2]
    entries = asrc_ref.shape[1]
    MESH = pl.DeviceIdType.MESH

    barrier = pltpu.get_barrier_semaphore()

    def greet(p, carry):
        @pl.when(p != me)
        def _():
            pl.semaphore_signal(
                barrier, inc=1, device_id={"tile": p // n_row, "row": p % n_row},
                device_id_type=MESH,
            )
        return carry

    lax.fori_loop(0, peers, greet, 0)
    pl.semaphore_signal(barrier, inc=1, device_id={"lev": 1 - lev}, device_id_type=MESH)

    lane16 = iota((16, LANE), 1)
    group16 = lane16 // 8

    def column_sum(state_ref, weights_ref, count):
        totals = [weights_ref[k] * state_ref[k] for k in range(4)]
        for k in range(4, count):
            totals[k % 4] = totals[k % 4] + weights_ref[k] * state_ref[k]
        return (totals[0] + totals[1]) + (totals[2] + totals[3])

    def strips(state_ref, count, base):
        for i in range((count + PER - 1) // PER):
            acc = jnp.zeros((16, LANE), F32)
            for j in range(PER):
                k = i * PER + j
                if k < count:
                    acc = jnp.where(group16 == j, turn(state_ref[k], 8 * j + 4, 1), acc)
            ext1[base + i, 8:24, LANE:2 * LANE] = acc

    def weight_of_flux(weights_ref, profile_ref, count):
        total = weights_ref[0] * profile_ref[0]
        for k in range(1, count):
            total = total + weights_ref[k] * profile_ref[k]
        return total

    lev_copy = pltpu.make_async_remote_copy(
        src_ref=lev_send, dst_ref=lev_recv, send_sem=lv_send, recv_sem=lv_recv,
        device_id={"lev": 1 - lev}, device_id_type=MESH,
    )
    for i in FIRST:
        fetch(i).wait()
    lev_send[0:16, :] = column_sum(air_ref, aw_ref, n_air)
    lev_send[16:32, :] = column_sum(sea_ref, ow_ref, n_sea)
    for i in SECOND:
        fetch(i).wait()
    lev_send[32:40, :] = jnp.zeros((8, LANE), F32) + weight_of_flux(aw_ref, ap_ref, n_air)
    lev_send[40:48, :] = jnp.zeros((8, LANE), F32) + weight_of_flux(ow_ref, op_ref, n_sea)
    pl.semaphore_wait(barrier, peers)
    lev_copy.start()

    strips(air_ref, n_air, 0)
    strips(sea_ref, n_sea, g_air)
    land_sea = mask_ref[...].astype(F32)
    ext1[planes, 8:24, LANE:2 * LANE] = ka_ref[...]
    ext1[planes + 1, 8:24, LANE:2 * LANE] = ea_ref[...]
    ext1[planes + 2, 8:24, LANE:2 * LANE] = land_sea * ko_ref[...]
    ext1[planes + 3, 8:24, LANE:2 * LANE] = land_sea * eo_ref[...]

    sub = iota((8, LANE), 0)
    upper = sub < 4

    def pack_rows(state_ref, count, base):
        for j in range(count // 2):
            a, b = state_ref[2 * j], state_ref[2 * j + 1]
            rows_send[0, base + j] = jnp.where(upper, a[0:8], turn(b[0:8], 4, 0))
            rows_send[1, base + j] = jnp.where(upper, turn(a[8:16], 4, 0), b[8:16])

    def exists(dt, dr):
        ok = jnp.bool_(True)
        if dt < 0:
            ok = ok & (t + dt >= 0)
        if dt > 0:
            ok = ok & (t + dt < n_tile)
        if dr < 0:
            ok = ok & (r + dr >= 0)
        if dr > 0:
            ok = ok & (r + dr < n_row)
        return ok

    def halo_copy(ext, send, recv, d):
        dt, dr = DIRS[d]
        source_rows = {-1: (8, 16), 0: (8, 24), 1: (16, 24)}[dt]
        target_rows = {-1: (24, 32), 0: (8, 24), 1: (0, 8)}[dt]
        target_lanes = {-1: 2 * LANE, 0: LANE, 1: 0}[dr]
        return pltpu.make_async_remote_copy(
            src_ref=ext.at[:, source_rows[0]:source_rows[1], LANE:2 * LANE],
            dst_ref=ext.at[:, target_rows[0]:target_rows[1], target_lanes:target_lanes + LANE],
            send_sem=send.at[d],
            recv_sem=recv.at[d],
            device_id={"tile": t + dt, "row": r + dr},
            device_id_type=MESH,
        )

    def halo_start(ext, send, recv):
        for d, (dt, dr) in enumerate(DIRS):
            @pl.when(exists(dt, dr))
            def _():
                halo_copy(ext, send, recv, d).start()

    def halo_clear(ext):
        for dt, dr in DIRS:
            rows = {-1: (24, 32), 0: (8, 24), 1: (0, 8)}[dt]
            lanes = {-1: 2 * LANE, 0: LANE, 1: 0}[dr]
            @pl.when(jnp.logical_not(exists(-dt, -dr)))
            def _():
                ext[:, rows[0]:rows[1], lanes:lanes + LANE] = jnp.zeros(
                    (ext.shape[0], rows[1] - rows[0], LANE), F32
                )

    def halo_wait_recv(ext, send, recv):
        for d, (dt, dr) in enumerate(DIRS):
            @pl.when(exists(-dt, -dr))
            def _():
                halo_copy(ext, send, recv, d).wait_recv()

    def halo_wait_send(ext, send, recv):
        for d, (dt, dr) in enumerate(DIRS):
            @pl.when(exists(dt, dr))
            def _():
                halo_copy(ext, send, recv, d).wait_send()

    def rows_copy(d):
        return pltpu.make_async_remote_copy(
            src_ref=rows_send.at[d], dst_ref=rows_recv.at[d],
            send_sem=rs_send.at[d], recv_sem=rs_recv.at[d],
            device_id={"tile": t + (1 if d else -1)}, device_id_type=MESH,
        )

    halo_start(ext1, send1, recv1)
    pack_rows(air_ref, n_air, 0)
    pack_rows(sea_ref, n_sea, n_air // 2)
    for d in range(2):
        @pl.when(exists(1 if d else -1, 0))
        def _():
            rows_copy(d).start()

        @pl.when(jnp.logical_not(exists(-1 if d else 1, 0)))
        def _():
            rows_recv[d] = jnp.zeros(rows_recv.shape[1:], F32)
    halo_clear(ext1)
    halo_clear(ext2)
    halo_clear(ext3)

    cells = 16 * LANE
    index_ref[...] = jnp.zeros(index_ref.shape, jnp.int32)
    index_ref[:, 0:cap] = asend_ref[0]
    index_ref[:, cap:2 * cap] = osend_ref[0] + cells
    index = index_ref[...]
    on_diagonal = iota((peers, peers), 0) == iota((peers, peers), 1)

    def live_count(counts_ref):
        counts = jnp.broadcast_to(counts_ref[...].astype(F32), (peers, peers))
        return jnp.sum(jnp.where(on_diagonal, counts, 0.0), axis=1, keepdims=True)

    slot_lane = iota((peers, LANE), 1)
    limit = jnp.where(slot_lane < cap, live_count(acnt_ref), live_count(ocnt_ref))
    limit = jnp.where(slot_lane < 2 * cap, limit, 0.0)
    live = (slot_lane % cap).astype(F32) < limit
    index_lane = index % LANE
    index_row = index // LANE

    lev_copy.wait_recv()
    surface = lev_send[...] + lev_recv[...]
    ext2[0, 8:24, LANE:2 * LANE] = surface[0:16]
    ext2[1, 8:24, LANE:2 * LANE] = surface[16:32]
    values = jnp.zeros((peers, LANE), F32)
    for x in range(32):
        row = jnp.broadcast_to(surface[x:x + 1], (peers, LANE))
        picked = jnp.take_along_axis(row, index_lane, axis=1, mode="promise_in_bounds")
        values = jnp.where(index_row == x, picked, values)
    values = jnp.where(live, values, 0.0)
    slot_send[...] = values.reshape(peers, 1, LANE)

    def slot_copy(p, recv_slot):
        return pltpu.make_async_remote_copy(
            src_ref=slot_send.at[p], dst_ref=slot_recv.at[recv_slot],
            send_sem=sl_send.at[p], recv_sem=sl_recv.at[recv_slot],
            device_id={"tile": p // n_row, "row": p % n_row}, device_id_type=MESH,
        )

    def others(action):
        def step(p, carry):
            @pl.when(p != me)
            def _():
                action(p)
            return carry
        lax.fori_loop(0, peers, step, 0)

    others(lambda p: slot_copy(p, me).start())
    halo_start(ext2, send2, recv2)
    slot_recv[me] = slot_send[me]

    cell_y = iota((LANE, LANE), 0)
    for m, tgt_ref in enumerate((atgt_ref, otgt_ref)):
        for c in range(entries // LANE):
            y = tgt_ref[0:1, c * LANE:(c + 1) * LANE] % LANE
            onehot_ref[m, :, c * LANE:(c + 1) * LANE] = jnp.where(
                jnp.broadcast_to(y, (LANE, LANE)) == cell_y, 1.0, 0.0
            ).astype(jnp.bfloat16)

    others(lambda p: slot_copy(p, p).wait_recv())
    table = slot_recv[...].reshape(peers, LANE)
    cell_x = iota((16, LANE), 0)
    sender = iota((peers, LANE), 0)
    for m, (src_ref, tgt_ref, shr_ref) in enumerate(
        ((asrc_ref, atgt_ref, ashr_ref), (osrc_ref, otgt_ref, oshr_ref))
    ):
        parts = ([], [], [])
        for c in range(entries // LANE):
            at = slice(c * LANE, (c + 1) * LANE)
            source = jnp.broadcast_to(src_ref[0:1, at], (peers, LANE))
            picked = jnp.take_along_axis(
                table, source % cap + m * cap, axis=1, mode="promise_in_bounds"
            )
            value = jnp.sum(jnp.where(source // cap == sender, picked, 0.0), axis=0, keepdims=True)
            value = value * shr_ref[0:1, at]
            x = jnp.broadcast_to(tgt_ref[0:1, at] // LANE, (16, LANE))
            spread = jnp.where(x == cell_x, jnp.broadcast_to(value, (16, LANE)), 0.0)
            high = spread.astype(jnp.bfloat16)
            rest = spread - high.astype(F32)
            middle = rest.astype(jnp.bfloat16)
            low = (rest - middle.astype(F32)).astype(jnp.bfloat16)
            parts[0].append(high)
            parts[1].append(middle)
            parts[2].append(low)
        left = jnp.concatenate([jnp.concatenate(p, axis=1) for p in parts], axis=0)
        product = lax.dot_general(
            left, onehot_ref[m], (((1,), (1,)), ((), ())), preferred_element_type=F32
        )
        ext3[1 - m, 8:24, LANE:2 * LANE] = product[0:16] + product[16:32] + product[32:48]
    halo_start(ext3, send3, recv3)

    halo_wait_recv(ext1, send1, recv1)
    for d in range(2):
        @pl.when(exists(-1 if d else 1, 0))
        def _():
            rows_copy(d).wait_recv()

    lane32 = iota((32, LANE), 1)
    low_lanes = lane32 < 8
    left_half = lane32 % 8 < 4
    lane24 = iota((24, LANE), 1)
    first_lane = lane24 == 0
    last_lane = lane24 == LANE - 1

    def advance(state_ref, out_ref, edge_ref, count, base, rows_base, plane, steps):
        kl = repeat_8(turn(ext1[plane, :, 0:LANE], 4, 1), low_lanes)
        kc = repeat_8(turn(ext1[plane, :, LANE:2 * LANE], 4, 1), low_lanes)
        kr = repeat_8(turn(ext1[plane, :, 2 * LANE:], 4, 1), low_lanes)
        kappa_left = jnp.where(left_half, kl, kc)
        kappa_right = jnp.where(left_half, kc, kr)
        kappa = ext1[plane, 4:28, LANE:2 * LANE]
        for i in range((count + PER - 1) // PER):
            own = ext1[base + i, :, LANE:2 * LANE]
            left = jnp.where(left_half, ext1[base + i, :, 0:LANE], own)
            right = jnp.where(left_half, own, ext1[base + i, :, 2 * LANE:])
            for n in range(steps):
                edge = jnp.where(lane32 % 8 == 3, left, turn(right, -2, 1))
                edge_ref[n, i] = edge[4:28]
                if n + 1 < steps:
                    left = left + kappa_left * lap_wrapped(left)
                    right = right + kappa_right * lap_wrapped(right)

        def group(h, carry):
            fields, places = [], []
            for b in range(levels):
                k = h * levels + b
                q = k // 2
                top, bottom = rows_recv[1, rows_base + q], rows_recv[0, rows_base + q]
                if b % 2:
                    top = turn(top, 4, 0)
                else:
                    bottom = turn(bottom, 4, 0)
                a = turn(state_ref[k, 0:8, :], 4, 0)
                c = turn(state_ref[k, 8:16, :], 4, 0)
                fields.append(jnp.concatenate(
                    [jnp.where(upper, top, a), jnp.where(upper, a, c), jnp.where(upper, c, bottom)],
                    axis=0,
                ))
                places.append((k // PER, (2 * LANE - 3 - 8 * (k % PER)) % LANE))
            for n in range(steps):
                for b in range(levels):
                    x = fields[b]
                    i, shift = places[b]
                    edge = pltpu.roll(edge_ref[n, i], shift, 1)
                    around = (
                        turn(x, 1, 0) + turn(x, -1, 0)
                        + jnp.where(first_lane, edge, turn(x, 1, 1))
                        + jnp.where(last_lane, edge, turn(x, -1, 1))
                    )
                    fields[b] = x + kappa * (around - 4.0 * x)
            for b in range(levels):
                x = fields[b]
                k = h * levels + b
                a, c, e = turn(x[0:8], 4, 0), turn(x[8:16], 4, 0), turn(x[16:24], 4, 0)
                out_ref[k, 0:8, :] = jnp.where(upper, a, c)
                out_ref[k, 8:16, :] = jnp.where(upper, c, e)
            return carry

        levels = max(v for v in (2, 4, 6, 8) if count % v == 0)
        lax.fori_loop(0, count // levels, group, 0)

    advance(air_ref, air_out, edge_air, n_air, 0, 0, planes, AIR_STEPS)
    advance(sea_ref, sea_out, edge_sea, n_sea, g_air, n_air // 2, planes + 2, SEA_STEPS)

    halo_wait_recv(ext2, send2, recv2)
    halo_wait_recv(ext3, send3, recv3)
    for m, (out_ref, profile_ref, count, steps) in enumerate(
        ((air_out, ap_ref, n_air, AIR_STEPS), (sea_out, op_ref, n_sea, SEA_STEPS))
    ):
        flux_weight = surface[32 + 8 * m:33 + 8 * m]
        flux_weight = jnp.concatenate([flux_weight] * 3, axis=1)
        kappa = ext1[planes + 2 * m]
        exchange = ext1[planes + 2 * m + 1]
        s = ext2[m]
        q = ext3[m]
        g = None
        for n in range(steps):
            flux = exchange * (q - s)
            g = flux if g is None else g + kappa * lap_wrapped(g) + flux
            if n + 1 < steps:
                s = s + kappa * lap_wrapped(s) + flux_weight * flux
        center = g[8:24, LANE:2 * LANE]
        for k in range(count):
            out_ref[k] = out_ref[k] + profile_ref[k] * center

    lev_copy.wait_send()
    others(lambda p: slot_copy(p, me).wait_send())
    halo_wait_send(ext1, send1, recv1)
    halo_wait_send(ext2, send2, recv2)
    halo_wait_send(ext3, send3, recv3)
    for d in range(2):
        @pl.when(exists(1 if d else -1, 0))
        def _():
            rows_copy(d).wait_send()


def body(*args):
    air, sea = args[0], args[5]
    n_air, n_sea = air.shape[0], sea.shape[0]
    n_tile, n_row = lax.axis_size("tile"), lax.axis_size("row")
    peers = n_tile * n_row
    entries = args[13].shape[1]
    g_air, g_sea = -(-n_air // PER), -(-n_sea // PER)
    vmem = pl.BlockSpec(memory_space=pltpu.VMEM)
    hbm = pl.BlockSpec(memory_space=pltpu.HBM)
    scalars = (3, 4, 9, 10)
    packed = (n_air + n_sea) // 2
    DMA = pltpu.SemaphoreType.DMA
    return pl.pallas_call(
        functools.partial(kernel, n_tile, n_row),
        out_shape=(
            jax.ShapeDtypeStruct(air.shape, F32),
            jax.ShapeDtypeStruct(sea.shape, F32),
        ),
        in_specs=[hbm] * len(args),
        out_specs=(vmem, vmem),
        scratch_shapes=[
            (pltpu.SMEM if i in scalars else pltpu.VMEM)(v.shape, v.dtype)
            for i, v in enumerate(args)
        ] + [
            DMA((len(args),)),
            pltpu.VMEM((g_air + g_sea + 4, 32, 3 * LANE), F32),
            pltpu.VMEM((2, 32, 3 * LANE), F32),
            pltpu.VMEM((2, 32, 3 * LANE), F32),
            pltpu.VMEM((2, packed, 8, LANE), F32),
            pltpu.VMEM((2, packed, 8, LANE), F32),
            pltpu.VMEM((48, LANE), F32),
            pltpu.VMEM((48, LANE), F32),
            pltpu.VMEM((peers, 1, LANE), F32),
            pltpu.VMEM((peers, 1, LANE), F32),
            pltpu.VMEM((peers, LANE), jnp.int32),
            pltpu.VMEM((2, LANE, entries), jnp.bfloat16),
            pltpu.VMEM((AIR_STEPS, g_air, 24, LANE), F32),
            pltpu.VMEM((SEA_STEPS, g_sea, 24, LANE), F32),
            DMA((8,)), DMA((8,)), DMA((8,)), DMA((8,)), DMA((8,)), DMA((8,)),
            DMA((2,)), DMA((2,)), DMA, DMA, DMA((peers,)), DMA((peers,)),
        ],
        compiler_params=pltpu.CompilerParams(
            collective_id=0, has_side_effects=True, vmem_limit_bytes=60 * 1024 * 1024
        ),
    )(*args)


def solution(mesh):
    field = P("lev", ("ens", "tile"), "row")
    cell = P(("ens", "tile"), "row")
    level = P("lev")
    table = P(("ens", "tile", "row"), None)
    lists = P(("ens", "tile", "row"), None, None)
    placed = (
        field, cell, cell, level, level,
        field, cell, cell, cell, level, level,
        table, lists, table, table, table,
        table, lists, table, table, table,
    )
    return jax.shard_map(
        body, mesh=mesh, in_specs=placed, out_specs=(field, field), check_vma=False
    )
```

```python
import functools

import jax
import jax.numpy as jnp
from jax import lax
from jax.experimental import pallas as pl
from jax.experimental.pallas import tpu as pltpu
from jax.sharding import PartitionSpec as P

AIR_STEPS = 4
SEA_STEPS = 2
F32 = jnp.float32
DIRS = tuple((dt, dr) for dt in (-1, 0, 1) for dr in (-1, 0, 1) if (dt, dr) != (0, 0))
LANE = 128
FIRST = (0, 5, 3, 9)
SECOND = (1, 2, 4, 6, 7, 8, 10, 11, 12, 13, 14, 15, 16, 17, 18, 19, 20)
PER = 16


def iota(shape, dim):
    return lax.broadcasted_iota(jnp.int32, shape, dim)


def turn(x, shift, axis):
    return pltpu.roll(x, shift % x.shape[axis], axis)


def lap_wrapped(x):
    return (
        turn(x, 1, 0) + turn(x, -1, 0) + turn(x, 1, 1) + turn(x, -1, 1) - 4.0 * x
    )


def repeat_8(x, low):
    y = jnp.where(low, x, 0.0)
    for width in (8, 16, 32, 64):
        y = y + turn(y, width, 1)
    return y


def kernel(n_tile, n_row, *refs):
    operands, (air_out, sea_out) = refs[:21], refs[21:23]
    held, rest = refs[23:44], refs[44:]
    (
        air_ref, ka_ref, ea_ref, aw_ref, ap_ref,
        sea_ref, ko_ref, eo_ref, mask_ref, ow_ref, op_ref,
        acnt_ref, asend_ref, asrc_ref, atgt_ref, ashr_ref,
        ocnt_ref, osend_ref, osrc_ref, otgt_ref, oshr_ref,
    ) = held
    (
        in_sem,
        ext1, ext2, ext3, rows_send, rows_recv, lev_send, lev_recv,
        slot_send, slot_recv, index_ref, onehot_ref, edge_air, edge_sea,
        send1, recv1, send2, recv2, send3, recv3,
        rs_send, rs_recv, lv_send, lv_recv, sl_send, sl_recv,
    ) = rest

    def fetch(i):
        return pltpu.make_async_copy(operands[i], held[i], in_sem.at[i])

    for i in FIRST + SECOND:
        fetch(i).start()

    t = lax.axis_index("tile")
    r = lax.axis_index("row")
    lev = lax.axis_index("lev")
    me = t * n_row + r
    peers = n_tile * n_row
    n_air = air_ref.shape[0]
    n_sea = sea_ref.shape[0]
    g_air = (n_air + PER - 1) // PER
    g_sea = (n_sea + PER - 1) // PER
    planes = g_air + g_sea
    cap = asend_ref.shape[2]
    entries = asrc_ref.shape[1]
    MESH = pl.DeviceIdType.MESH

    barrier = pltpu.get_barrier_semaphore()

    def greet(p, carry):
        @pl.when(p != me)
        def _():
            pl.semaphore_signal(
                barrier, inc=1, device_id={"tile": p // n_row, "row": p % n_row},
                device_id_type=MESH,
            )
        return carry

    lax.fori_loop(0, peers, greet, 0)
    pl.semaphore_signal(barrier, inc=1, device_id={"lev": 1 - lev}, device_id_type=MESH)

    lane16 = iota((16, LANE), 1)
    group16 = lane16 // 8

    def column_sum(state_ref, weights_ref, count):
        totals = [weights_ref[k] * state_ref[k] for k in range(4)]
        for k in range(4, count):
            totals[k % 4] = totals[k % 4] + weights_ref[k] * state_ref[k]
        return (totals[0] + totals[1]) + (totals[2] + totals[3])

    def strips(state_ref, count, base):
        for i in range((count + PER - 1) // PER):
            acc = jnp.zeros((16, LANE), F32)
            for j in range(PER):
                k = i * PER + j
                if k < count:
                    acc = jnp.where(group16 == j, turn(state_ref[k], 8 * j + 4, 1), acc)
            ext1[base + i, 8:24, LANE:2 * LANE] = acc

    def weight_of_flux(weights_ref, profile_ref, count):
        total = weights_ref[0] * profile_ref[0]
        for k in range(1, count):
            total = total + weights_ref[k] * profile_ref[k]
        return total

    lev_copy = pltpu.make_async_remote_copy(
        src_ref=lev_send, dst_ref=lev_recv, send_sem=lv_send, recv_sem=lv_recv,
        device_id={"lev": 1 - lev}, device_id_type=MESH,
    )
    for i in FIRST:
        fetch(i).wait()
    lev_send[0:16, :] = column_sum(air_ref, aw_ref, n_air)
    lev_send[16:32, :] = column_sum(sea_ref, ow_ref, n_sea)
    for i in (4, 10):
        fetch(i).wait()
    lev_send[32:40, :] = jnp.zeros((8, LANE), F32) + weight_of_flux(aw_ref, ap_ref, n_air)
    lev_send[40:48, :] = jnp.zeros((8, LANE), F32) + weight_of_flux(ow_ref, op_ref, n_sea)
    pl.semaphore_wait(barrier, peers)
    lev_copy.start()
    for i in SECOND:
        if i not in (4, 10):
            fetch(i).wait()

    strips(air_ref, n_air, 0)
    strips(sea_ref, n_sea, g_air)
    land_sea = mask_ref[...].astype(F32)
    ext1[planes, 8:24, LANE:2 * LANE] = ka_ref[...]
    ext1[planes + 1, 8:24, LANE:2 * LANE] = ea_ref[...]
    ext1[planes + 2, 8:24, LANE:2 * LANE] = land_sea * ko_ref[...]
    ext1[planes + 3, 8:24, LANE:2 * LANE] = land_sea * eo_ref[...]

    sub = iota((8, LANE), 0)
    upper = sub < 4

    def pack_rows(state_ref, count, base):
        for j in range(count // 2):
            a, b = state_ref[2 * j], state_ref[2 * j + 1]
            rows_send[0, base + j] = jnp.where(upper, a[0:8], turn(b[0:8], 4, 0))
            rows_send[1, base + j] = jnp.where(upper, turn(a[8:16], 4, 0), b[8:16])

    def exists(dt, dr):
        ok = jnp.bool_(True)
        if dt < 0:
            ok = ok & (t + dt >= 0)
        if dt > 0:
            ok = ok & (t + dt < n_tile)
        if dr < 0:
            ok = ok & (r + dr >= 0)
        if dr > 0:
            ok = ok & (r + dr < n_row)
        return ok

    def halo_copy(ext, send, recv, d):
        dt, dr = DIRS[d]
        source_rows = {-1: (8, 16), 0: (8, 24), 1: (16, 24)}[dt]
        target_rows = {-1: (24, 32), 0: (8, 24), 1: (0, 8)}[dt]
        target_lanes = {-1: 2 * LANE, 0: LANE, 1: 0}[dr]
        return pltpu.make_async_remote_copy(
            src_ref=ext.at[:, source_rows[0]:source_rows[1], LANE:2 * LANE],
            dst_ref=ext.at[:, target_rows[0]:target_rows[1], target_lanes:target_lanes + LANE],
            send_sem=send.at[d],
            recv_sem=recv.at[d],
            device_id={"tile": t + dt, "row": r + dr},
            device_id_type=MESH,
        )

    def halo_start(ext, send, recv):
        for d, (dt, dr) in enumerate(DIRS):
            @pl.when(exists(dt, dr))
            def _():
                halo_copy(ext, send, recv, d).start()

    def halo_clear(ext):
        for dt, dr in DIRS:
            rows = {-1: (24, 32), 0: (8, 24), 1: (0, 8)}[dt]
            lanes = {-1: 2 * LANE, 0: LANE, 1: 0}[dr]
            @pl.when(jnp.logical_not(exists(-dt, -dr)))
            def _():
                ext[:, rows[0]:rows[1], lanes:lanes + LANE] = jnp.zeros(
                    (ext.shape[0], rows[1] - rows[0], LANE), F32
                )

    def halo_wait_recv(ext, send, recv):
        for d, (dt, dr) in enumerate(DIRS):
            @pl.when(exists(-dt, -dr))
            def _():
                halo_copy(ext, send, recv, d).wait_recv()

    def halo_wait_send(ext, send, recv):
        for d, (dt, dr) in enumerate(DIRS):
            @pl.when(exists(dt, dr))
            def _():
                halo_copy(ext, send, recv, d).wait_send()

    def rows_copy(d):
        return pltpu.make_async_remote_copy(
            src_ref=rows_send.at[d], dst_ref=rows_recv.at[d],
            send_sem=rs_send.at[d], recv_sem=rs_recv.at[d],
            device_id={"tile": t + (1 if d else -1)}, device_id_type=MESH,
        )

    halo_start(ext1, send1, recv1)
    pack_rows(air_ref, n_air, 0)
    pack_rows(sea_ref, n_sea, n_air // 2)
    for d in range(2):
        @pl.when(exists(1 if d else -1, 0))
        def _():
            rows_copy(d).start()

        @pl.when(jnp.logical_not(exists(-1 if d else 1, 0)))
        def _():
            rows_recv[d] = jnp.zeros(rows_recv.shape[1:], F32)
    halo_clear(ext1)
    halo_clear(ext2)
    halo_clear(ext3)

    cells = 16 * LANE
    index_ref[...] = jnp.zeros(index_ref.shape, jnp.int32)
    index_ref[:, 0:cap] = asend_ref[0]
    index_ref[:, cap:2 * cap] = osend_ref[0] + cells
    index = index_ref[...]
    on_diagonal = iota((peers, peers), 0) == iota((peers, peers), 1)

    def live_count(counts_ref):
        counts = jnp.broadcast_to(counts_ref[...].astype(F32), (peers, peers))
        return jnp.sum(jnp.where(on_diagonal, counts, 0.0), axis=1, keepdims=True)

    slot_lane = iota((peers, LANE), 1)
    limit = jnp.where(slot_lane < cap, live_count(acnt_ref), live_count(ocnt_ref))
    limit = jnp.where(slot_lane < 2 * cap, limit, 0.0)
    live = (slot_lane % cap).astype(F32) < limit
    index_lane = index % LANE
    index_row = index // LANE

    lev_copy.wait_recv()
    surface = lev_send[...] + lev_recv[...]
    ext2[0, 8:24, LANE:2 * LANE] = surface[0:16]
    ext2[1, 8:24, LANE:2 * LANE] = surface[16:32]
    values = jnp.zeros((peers, LANE), F32)
    for x in range(32):
        row = jnp.broadcast_to(surface[x:x + 1], (peers, LANE))
        picked = jnp.take_along_axis(row, index_lane, axis=1, mode="promise_in_bounds")
        values = jnp.where(index_row == x, picked, values)
    values = jnp.where(live, values, 0.0)
    slot_send[...] = values.reshape(peers, 1, LANE)

    def slot_copy(p, recv_slot):
        return pltpu.make_async_remote_copy(
            src_ref=slot_send.at[p], dst_ref=slot_recv.at[recv_slot],
            send_sem=sl_send.at[p], recv_sem=sl_recv.at[recv_slot],
            device_id={"tile": p // n_row, "row": p % n_row}, device_id_type=MESH,
        )

    def others(action):
        def step(p, carry):
            @pl.when(p != me)
            def _():
                action(p)
            return carry
        lax.fori_loop(0, peers, step, 0)

    others(lambda p: slot_copy(p, me).start())
    halo_start(ext2, send2, recv2)
    slot_recv[me] = slot_send[me]

    cell_y = iota((LANE, LANE), 0)
    for m, tgt_ref in enumerate((atgt_ref, otgt_ref)):
        for c in range(entries // LANE):
            y = tgt_ref[0:1, c * LANE:(c + 1) * LANE] % LANE
            onehot_ref[m, :, c * LANE:(c + 1) * LANE] = jnp.where(
                jnp.broadcast_to(y, (LANE, LANE)) == cell_y, 1.0, 0.0
            ).astype(jnp.bfloat16)

    others(lambda p: slot_copy(p, p).wait_recv())
    table = slot_recv[...].reshape(peers, LANE)
    cell_x = iota((16, LANE), 0)
    sender = iota((peers, LANE), 0)
    for m, (src_ref, tgt_ref, shr_ref) in enumerate(
        ((asrc_ref, atgt_ref, ashr_ref), (osrc_ref, otgt_ref, oshr_ref))
    ):
        parts = ([], [], [])
        for c in range(entries // LANE):
            at = slice(c * LANE, (c + 1) * LANE)
            source = jnp.broadcast_to(src_ref[0:1, at], (peers, LANE))
            picked = jnp.take_along_axis(
                table, source % cap + m * cap, axis=1, mode="promise_in_bounds"
            )
            value = jnp.sum(jnp.where(source // cap == sender, picked, 0.0), axis=0, keepdims=True)
            value = value * shr_ref[0:1, at]
            x = jnp.broadcast_to(tgt_ref[0:1, at] // LANE, (16, LANE))
            spread = jnp.where(x == cell_x, jnp.broadcast_to(value, (16, LANE)), 0.0)
            high = spread.astype(jnp.bfloat16)
            rest = spread - high.astype(F32)
            middle = rest.astype(jnp.bfloat16)
            low = (rest - middle.astype(F32)).astype(jnp.bfloat16)
            parts[0].append(high)
            parts[1].append(middle)
            parts[2].append(low)
        left = jnp.concatenate([jnp.concatenate(p, axis=1) for p in parts], axis=0)
        product = lax.dot_general(
            left, onehot_ref[m], (((1,), (1,)), ((), ())), preferred_element_type=F32
        )
        ext3[1 - m, 8:24, LANE:2 * LANE] = product[0:16] + product[16:32] + product[32:48]
    halo_start(ext3, send3, recv3)

    halo_wait_recv(ext1, send1, recv1)
    for d in range(2):
        @pl.when(exists(-1 if d else 1, 0))
        def _():
            rows_copy(d).wait_recv()

    lane32 = iota((32, LANE), 1)
    low_lanes = lane32 < 8
    left_half = lane32 % 8 < 4
    lane24 = iota((24, LANE), 1)
    first_lane = lane24 == 0
    last_lane = lane24 == LANE - 1

    def advance(state_ref, out_ref, edge_ref, count, base, rows_base, plane, steps):
        kl = repeat_8(turn(ext1[plane, :, 0:LANE], 4, 1), low_lanes)
        kc = repeat_8(turn(ext1[plane, :, LANE:2 * LANE], 4, 1), low_lanes)
        kr = repeat_8(turn(ext1[plane, :, 2 * LANE:], 4, 1), low_lanes)
        kappa_left = jnp.where(left_half, kl, kc)
        kappa_right = jnp.where(left_half, kc, kr)
        kappa = ext1[plane, 4:28, LANE:2 * LANE]
        for i in range((count + PER - 1) // PER):
            own = ext1[base + i, :, LANE:2 * LANE]
            left = jnp.where(left_half, ext1[base + i, :, 0:LANE], own)
            right = jnp.where(left_half, own, ext1[base + i, :, 2 * LANE:])
            for n in range(steps):
                edge = jnp.where(lane32 % 8 == 3, left, turn(right, -2, 1))
                edge_ref[n, i] = edge[4:28]
                if n + 1 < steps:
                    left = left + kappa_left * lap_wrapped(left)
                    right = right + kappa_right * lap_wrapped(right)

        def group(h, carry):
            fields, places = [], []
            for b in range(levels):
                k = h * levels + b
                q = k // 2
                top, bottom = rows_recv[1, rows_base + q], rows_recv[0, rows_base + q]
                if b % 2:
                    top = turn(top, 4, 0)
                else:
                    bottom = turn(bottom, 4, 0)
                a = turn(state_ref[k, 0:8, :], 4, 0)
                c = turn(state_ref[k, 8:16, :], 4, 0)
                fields.append(jnp.concatenate(
                    [jnp.where(upper, top, a), jnp.where(upper, a, c), jnp.where(upper, c, bottom)],
                    axis=0,
                ))
                places.append((k // PER, (2 * LANE - 3 - 8 * (k % PER)) % LANE))
            for n in range(steps):
                for b in range(levels):
                    x = fields[b]
                    i, shift = places[b]
                    edge = pltpu.roll(edge_ref[n, i], shift, 1)
                    around = (
                        turn(x, 1, 0) + turn(x, -1, 0)
                        + jnp.where(first_lane, edge, turn(x, 1, 1))
                        + jnp.where(last_lane, edge, turn(x, -1, 1))
                    )
                    fields[b] = x + kappa * (around - 4.0 * x)
            for b in range(levels):
                x = fields[b]
                k = h * levels + b
                a, c, e = turn(x[0:8], 4, 0), turn(x[8:16], 4, 0), turn(x[16:24], 4, 0)
                out_ref[k, 0:8, :] = jnp.where(upper, a, c)
                out_ref[k, 8:16, :] = jnp.where(upper, c, e)
            return carry

        levels = max(v for v in (2, 4, 6, 8) if count % v == 0)
        lax.fori_loop(0, count // levels, group, 0)

    advance(air_ref, air_out, edge_air, n_air, 0, 0, planes, AIR_STEPS)
    advance(sea_ref, sea_out, edge_sea, n_sea, g_air, n_air // 2, planes + 2, SEA_STEPS)

    halo_wait_recv(ext2, send2, recv2)
    halo_wait_recv(ext3, send3, recv3)
    for m, (out_ref, profile_ref, count, steps) in enumerate(
        ((air_out, ap_ref, n_air, AIR_STEPS), (sea_out, op_ref, n_sea, SEA_STEPS))
    ):
        flux_weight = surface[32 + 8 * m:33 + 8 * m]
        flux_weight = jnp.concatenate([flux_weight] * 3, axis=1)
        kappa = ext1[planes + 2 * m]
        exchange = ext1[planes + 2 * m + 1]
        s = ext2[m]
        q = ext3[m]
        g = None
        for n in range(steps):
            flux = exchange * (q - s)
            g = flux if g is None else g + kappa * lap_wrapped(g) + flux
            if n + 1 < steps:
                s = s + kappa * lap_wrapped(s) + flux_weight * flux
        center = g[8:24, LANE:2 * LANE]
        for k in range(count):
            out_ref[k] = out_ref[k] + profile_ref[k] * center

    lev_copy.wait_send()
    others(lambda p: slot_copy(p, me).wait_send())
    halo_wait_send(ext1, send1, recv1)
    halo_wait_send(ext2, send2, recv2)
    halo_wait_send(ext3, send3, recv3)
    for d in range(2):
        @pl.when(exists(1 if d else -1, 0))
        def _():
            rows_copy(d).wait_send()


def body(*args):
    air, sea = args[0], args[5]
    n_air, n_sea = air.shape[0], sea.shape[0]
    n_tile, n_row = lax.axis_size("tile"), lax.axis_size("row")
    peers = n_tile * n_row
    entries = args[13].shape[1]
    g_air, g_sea = -(-n_air // PER), -(-n_sea // PER)
    vmem = pl.BlockSpec(memory_space=pltpu.VMEM)
    hbm = pl.BlockSpec(memory_space=pltpu.HBM)
    scalars = (3, 4, 9, 10)
    packed = (n_air + n_sea) // 2
    DMA = pltpu.SemaphoreType.DMA
    return pl.pallas_call(
        functools.partial(kernel, n_tile, n_row),
        out_shape=(
            jax.ShapeDtypeStruct(air.shape, F32),
            jax.ShapeDtypeStruct(sea.shape, F32),
        ),
        in_specs=[hbm] * len(args),
        out_specs=(vmem, vmem),
        scratch_shapes=[
            (pltpu.SMEM if i in scalars else pltpu.VMEM)(v.shape, v.dtype)
            for i, v in enumerate(args)
        ] + [
            DMA((len(args),)),
            pltpu.VMEM((g_air + g_sea + 4, 32, 3 * LANE), F32),
            pltpu.VMEM((2, 32, 3 * LANE), F32),
            pltpu.VMEM((2, 32, 3 * LANE), F32),
            pltpu.VMEM((2, packed, 8, LANE), F32),
            pltpu.VMEM((2, packed, 8, LANE), F32),
            pltpu.VMEM((48, LANE), F32),
            pltpu.VMEM((48, LANE), F32),
            pltpu.VMEM((peers, 1, LANE), F32),
            pltpu.VMEM((peers, 1, LANE), F32),
            pltpu.VMEM((peers, LANE), jnp.int32),
            pltpu.VMEM((2, LANE, entries), jnp.bfloat16),
            pltpu.VMEM((AIR_STEPS, g_air, 24, LANE), F32),
            pltpu.VMEM((SEA_STEPS, g_sea, 24, LANE), F32),
            DMA((8,)), DMA((8,)), DMA((8,)), DMA((8,)), DMA((8,)), DMA((8,)),
            DMA((2,)), DMA((2,)), DMA, DMA, DMA((peers,)), DMA((peers,)),
        ],
        compiler_params=pltpu.CompilerParams(
            collective_id=0, has_side_effects=True, vmem_limit_bytes=60 * 1024 * 1024
        ),
    )(*args)


def solution(mesh):
    field = P("lev", ("ens", "tile"), "row")
    cell = P(("ens", "tile"), "row")
    level = P("lev")
    table = P(("ens", "tile", "row"), None)
    lists = P(("ens", "tile", "row"), None, None)
    placed = (
        field, cell, cell, level, level,
        field, cell, cell, cell, level, level,
        table, lists, table, table, table,
        table, lists, table, table, table,
    )
    return jax.shard_map(
        body, mesh=mesh, in_specs=placed, out_specs=(field, field), check_vma=False
    )
```
